256 devices in a mesh: section: 32 (over y, z_hi, core), tensor: 8 (over x, z_lo).
Axes of the slice: x: 4, y: 4, z: 8 (z_hi: 4, z_lo: 2; z = z_hi * 2 + z_lo), core: 2. Of those that a mesh axis runs over, the one named last changes fastest.
Arguments:
- inflow: float32 [32, 256, 4096], P('section', 'tensor'), may hold values from -6 to 6
- fresh: float32 [256, 4096], P('tensor'), may hold values from -6 to 6
- states: float32 [32, 8, 256, 256], P('section', 'tensor'), may hold values from -1.5 to 1.5
- rates: float32 [32, 8], P('section', 'tensor'), may hold values from 0.00024414062 to 0.03125
- norm_gain: float32 [32, 4096], P('section'), may hold values from 0.1 to 1.9
- w_query: bfloat16 [32, 4096, 2048], P('section', None, 'tensor'), may hold values from -0.09375 to 0.09375
- w_key: bfloat16 [32, 4096, 2048], P('section', None, 'tensor'), may hold values from -0.09375 to 0.09375
- w_value: bfloat16 [32, 4096, 2048], P('section', None, 'tensor'), may hold values from -0.09375 to 0.09375
- w_gate: bfloat16 [32, 4096, 2048], P('section', None, 'tensor'), may hold values from -0.09375 to 0.09375
- w_out: bfloat16 [32, 2048, 4096], P('section', 'tensor'), may hold values from -0.125 to 0.125
Outputs:
- outflow: float32 [32, 256, 4096], P('section', 'tensor')
- final_states: float32 [32, 8, 256, 256], P('section', 'tensor')
The draws below stay inside these ranges and needn't reach their ends.
All inputs are finite; a program needn't handle non-finite values.
Results may differ from the reference program's by a relative error of at most 0.02.
Values may be sent and summed in bfloat16 or wider, within the bound.
No kernel may reach another device: no remote copies, remote signals or barrier semaphores. Data moves between devices by JAX's collectives and lax.ppermute only.
A program may use at most 128 MiB of HBM per device.

```python
import math
import jax
import jax.numpy as jnp
from jax import lax

D = 4096
HEADS = 8
DK = 256
DV = 256
GROUP = 256
SECTIONS = 32


def block_scale(key, dims, split, low, largest):
    level = 1.0
    for position, parts in split:
        heights = jax.random.uniform(jax.random.fold_in(jax.random.fold_in(key, 6), position), (parts,), jnp.float32, low / len(split), largest / len(split))
        level = level * jnp.repeat(jnp.exp(heights), dims[position] // parts).reshape((-1,) + (1,) * (len(dims) - 1 - position))
    return level


def bell_draw(rng, extent, scale, most, split=(), held_as=jnp.bfloat16):
    entries = jax.random.normal(rng, extent, jnp.float32) * scale
    if len(split) > 0:
        entries = block_scale(rng, extent, split, -0.22, 0.18) * entries
    return jnp.clip(entries, min=-most, max=most).astype(held_as)


def setup_inputs(seed: int = 0) -> dict:
    key_of = jax.random.split(jax.random.key(seed), 11)
    return {
        "inflow": bell_draw(key_of[0], (SECTIONS, GROUP, D), 1.0, 6.0, ((0, 32), (1, 8)), jnp.float32),
        "fresh": bell_draw(key_of[1], (GROUP, D), 1.0, 6.0, ((0, 8),), jnp.float32),
        "states": bell_draw(key_of[2], (SECTIONS, HEADS, DK, DV), 0.25, 1.5, ((0, 32), (1, 8)), jnp.float32),
        "rates": jnp.clip(jnp.exp(math.log(0.03125) - 4.8520303 * jax.random.uniform(key_of[3], (SECTIONS, HEADS), jnp.float32) ** block_scale(key_of[3], (SECTIONS, HEADS), ((0, 32), (1, 8)), -0.2, 0.2)), 0.00024414062, 0.03125),
        "norm_gain": jnp.clip(1.0 + 0.18 * jax.random.normal(key_of[4], (SECTIONS, D), jnp.float32), 0.1, 1.9),
        "w_query": bell_draw(key_of[5], (SECTIONS, D, HEADS * DK), D ** -0.5, 0.09375, ((0, 32), (2, 8))),
        "w_key": bell_draw(key_of[6], (SECTIONS, D, HEADS * DK), D ** -0.5, 0.09375, ((0, 32), (2, 8))),
        "w_value": bell_draw(key_of[7], (SECTIONS, D, HEADS * DV), D ** -0.5, 0.09375, ((0, 32), (2, 8))),
        "w_gate": bell_draw(key_of[8], (SECTIONS, D, HEADS * DV), D ** -0.5, 0.09375, ((0, 32), (2, 8))),
        "w_out": bell_draw(key_of[9], (SECTIONS, HEADS * DV, D), (HEADS * DV) ** -0.5, 0.125, ((0, 32), (1, 8))),
    }


EPSILON = 1e-05

def layer_norm(token_rows, gain_values):
    centred = token_rows - lax.optimization_barrier(jnp.mean(token_rows, axis=-1, keepdims=True))
    spread = lax.optimization_barrier(jnp.mean(centred * centred, axis=-1, keepdims=True))
    return (centred * lax.rsqrt(spread + EPSILON) * gain_values).astype(jnp.bfloat16)

def project(normed, query_weight, key_weight, value_weight, gate_weight):
    return jnp.concatenate([jnp.dot(normed, query_weight, preferred_element_type=jnp.float32), jnp.dot(normed, key_weight, preferred_element_type=jnp.float32), jnp.dot(normed, value_weight, preferred_element_type=jnp.float32), jnp.dot(normed, gate_weight, preferred_element_type=jnp.float32)], axis=1)

def retain(projected, state_now, rate_values, key_size, value_size):
    head_count = rate_values.shape[0]
    group_len = projected.shape[0]
    key_width = head_count * key_size
    value_width = head_count * value_size
    queries = projected[:, :key_width].astype(jnp.bfloat16).reshape(group_len, head_count, key_size)
    keys = (projected[:, key_width:2 * key_width] * key_size ** (-0.5)).astype(jnp.bfloat16).reshape(group_len, head_count, key_size)
    values = projected[:, 2 * key_width:2 * key_width + value_width].astype(jnp.bfloat16).reshape(group_len, head_count, value_size)
    gates = projected[:, 2 * key_width + value_width:]
    log_keep = jnp.log1p(-rate_values)
    positions = jnp.arange(group_len).astype(jnp.float32)
    offsets = positions[:, None] - positions[None, :]
    decay_mask = jnp.where(offsets[None] >= 0, jnp.exp(jnp.maximum(offsets, 0.0)[None] * log_keep[:, None, None]), 0.0)
    scores = jnp.einsum('ihd,jhd->hij', queries.astype(jnp.float32), keys.astype(jnp.float32))
    weighted = (scores * decay_mask).astype(jnp.bfloat16)
    inner = jnp.einsum('hij,jhe->ihe', weighted.astype(jnp.float32), values.astype(jnp.float32))
    carried = jnp.einsum('ihd,hde->ihe', queries.astype(jnp.float32), state_now, precision=lax.Precision.HIGHEST)
    carried = carried * jnp.exp((positions + 1.0)[:, None] * log_keep[None, :])[:, :, None]
    mixed = inner + carried
    centred = mixed - lax.optimization_barrier(jnp.mean(mixed, axis=-1, keepdims=True))
    head_out = centred * lax.rsqrt(lax.optimization_barrier(jnp.mean(centred * centred, axis=-1, keepdims=True)) + EPSILON)
    gated = (jax.nn.silu(gates).reshape(group_len, head_count, value_size) * head_out).reshape(group_len, value_width).astype(jnp.bfloat16)
    tail = jnp.exp((group_len - 1.0 - positions)[:, None] * log_keep[None, :])
    new_state = jnp.exp(group_len * log_keep)[:, None, None] * state_now + jnp.einsum('jhd,jhe->hde', keys.astype(jnp.float32) * tail[:, :, None], values.astype(jnp.float32), precision=lax.Precision.HIGHEST)
    return (gated, new_state)

def layer(packed):
    entering, state_now, rate_values, gain_values, query_weight, key_weight, value_weight, gate_weight, out_weight = packed
    projected = project(layer_norm(entering, gain_values), query_weight, key_weight, value_weight, gate_weight)
    gated, new_state = retain(projected, state_now, rate_values, state_now.shape[1], state_now.shape[2])
    return (entering + jnp.dot(gated, out_weight, preferred_element_type=jnp.float32), new_state)

def reference(inflow, fresh, states, rates, norm_gain, w_query, w_key, w_value, w_gate, w_out):
    first_out, first_states = lax.map(layer, (inflow, states, rates, norm_gain, w_query, w_key, w_value, w_gate, w_out))
    second_in = jnp.concatenate([fresh[None], first_out[:-1]], axis=0)
    outflow, final_states = lax.map(layer, (second_in, first_states, rates, norm_gain, w_query, w_key, w_value, w_gate, w_out))
    return (outflow, final_states)
```

```python
import jax
import jax.numpy as jnp
from jax import lax
from jax.sharding import PartitionSpec as P

EPSILON = 1e-05


def from_behind(value, axis, steps):
    count = lax.axis_size(axis)
    leading, last = (max(0, -steps), min(count, count - steps))
    return lax.ppermute(value, axis, [(source, source + steps) for source in range(leading, last)])


def layer_norm(token_rows, gain_values):
    centred = token_rows - jnp.mean(token_rows, axis=-1, keepdims=True)
    spread = jnp.mean(centred * centred, axis=-1, keepdims=True)
    return (centred * lax.rsqrt(spread + EPSILON) * gain_values).astype(jnp.bfloat16)


def project(normed, query_weight, key_weight, value_weight, gate_weight):
    return jnp.concatenate(
        [
            jnp.dot(normed, query_weight, preferred_element_type=jnp.float32),
            jnp.dot(normed, key_weight, preferred_element_type=jnp.float32),
            jnp.dot(normed, value_weight, preferred_element_type=jnp.float32),
            jnp.dot(normed, gate_weight, preferred_element_type=jnp.float32),
        ],
        axis=1,
    )


def retain(projected, state_now, rate_values, key_size, value_size):
    head_count = rate_values.shape[0]
    group_len = projected.shape[0]
    key_width = head_count * key_size
    value_width = head_count * value_size
    queries = projected[:, :key_width].astype(jnp.bfloat16).reshape(group_len, head_count, key_size)
    keys = (
        (projected[:, key_width : 2 * key_width] * key_size ** (-0.5))
        .astype(jnp.bfloat16)
        .reshape(group_len, head_count, key_size)
    )
    values = (
        projected[:, 2 * key_width : 2 * key_width + value_width]
        .astype(jnp.bfloat16)
        .reshape(group_len, head_count, value_size)
    )
    gates = projected[:, 2 * key_width + value_width :]
    log_keep = jnp.log1p(-rate_values)
    positions = jnp.arange(group_len).astype(jnp.float32)
    offsets = positions[:, None] - positions[None, :]
    decay_mask = jnp.where(
        offsets[None] >= 0, jnp.exp(jnp.maximum(offsets, 0.0)[None] * log_keep[:, None, None]), 0.0
    )
    scores = jnp.einsum("ihd,jhd->hij", queries, keys, preferred_element_type=jnp.float32)
    weighted = (scores * decay_mask).astype(jnp.bfloat16)
    inner = jnp.einsum("hij,jhe->ihe", weighted, values, preferred_element_type=jnp.float32)
    carried = jnp.einsum(
        "ihd,hde->ihe", queries.astype(jnp.float32), state_now, precision=lax.Precision.HIGHEST
    )
    carried = carried * jnp.exp((positions + 1.0)[:, None] * log_keep[None, :])[:, :, None]
    mixed = inner + carried
    centred = mixed - jnp.mean(mixed, axis=-1, keepdims=True)
    head_out = centred * lax.rsqrt(jnp.mean(centred * centred, axis=-1, keepdims=True) + EPSILON)
    gated = (
        (jax.nn.silu(gates).reshape(group_len, head_count, value_size) * head_out)
        .reshape(group_len, value_width)
        .astype(jnp.bfloat16)
    )
    tail = jnp.exp((group_len - 1.0 - positions)[:, None] * log_keep[None, :])
    new_state = jnp.exp(group_len * log_keep)[:, None, None] * state_now + jnp.einsum(
        "jhd,jhe->hde",
        keys.astype(jnp.float32) * tail[:, :, None],
        values.astype(jnp.float32),
        precision=lax.Precision.HIGHEST,
    )
    return (gated, new_state)


def gather_rows(rows):
    everywhere = jnp.broadcast_to(rows[None], (lax.axis_size("tensor"),) + rows.shape)
    return lax.all_to_all(everywhere, "tensor", 0, 0, tiled=True).reshape(-1, rows.shape[-1])


def scatter_sum(partial):
    count = lax.axis_size("tensor")
    parts = partial.reshape(count, partial.shape[0] // count, partial.shape[1])
    arrived = lax.all_to_all(parts, "tensor", 0, 0, tiled=True)
    return jnp.sum(arrived.astype(jnp.float32), axis=0)


def body(inflow, fresh, states, rates, norm_gain, w_query, w_key, w_value, w_gate, w_out):
    key_size = states.shape[2]
    value_size = states.shape[3]
    gain_here = norm_gain[0]
    rate_here = rates[0]
    state_now = states[0]
    out_here = w_out[0]
    first_section = lax.axis_index("section") == 0
    own_rows = inflow[0]
    for turn_index in range(2):
        normed = gather_rows(layer_norm(own_rows, gain_here))
        projected = project(normed, w_query[0], w_key[0], w_value[0], w_gate[0])
        gated, state_now = retain(projected, state_now, rate_here, key_size, value_size)
        partial = jnp.dot(gated, out_here, preferred_element_type=jnp.float32).astype(jnp.bfloat16)
        own_rows = own_rows + scatter_sum(partial)
        if turn_index == 0:
            arrived = from_behind(own_rows.astype(jnp.bfloat16), "section", 1)
            own_rows = jnp.where(first_section, fresh, arrived.astype(jnp.float32))
    return (own_rows[None], state_now[None])


def solution(mesh):
    in_specs = (
        P("section", "tensor", None),
        P("tensor", None),
        P("section", "tensor", None, None),
        P("section", "tensor"),
        P("section", None),
        P("section", None, "tensor"),
        P("section", None, "tensor"),
        P("section", None, "tensor"),
        P("section", None, "tensor"),
        P("section", "tensor", None),
    )
    out_specs = (P("section", "tensor", None), P("section", "tensor", None, None))
    return jax.shard_map(body, mesh=mesh, in_specs=in_specs, out_specs=out_specs, check_vma=False)
```

```python
import jax
import jax.numpy as jnp
from jax import lax
from jax.experimental import pallas as pl
from jax.experimental.pallas import tpu as pltpu
from jax.sharding import PartitionSpec as P

EPSILON = 1e-05
VMEM = pl.BlockSpec(memory_space=pltpu.VMEM)
SMEM = pl.BlockSpec(memory_space=pltpu.SMEM)
LIMIT = 16 * 1024 * 1024


def shift_x(value, steps):
    return lax.ppermute(value, "tensor", [(t, (t + 2 * steps) % 8) for t in range(8)])


def swap_z(value):
    return lax.ppermute(value, "tensor", [(t, t ^ 1) for t in range(8)])


def next_section(value):
    return lax.ppermute(value, "section", [(s, s + 1) for s in range(lax.axis_size("section") - 1)])


def call(kernel, out_shape, in_specs, flops=0, moved=0, scratch=()):
    return pl.pallas_call(
        kernel,
        out_shape=out_shape,
        in_specs=in_specs,
        out_specs=jax.tree.map(lambda _: VMEM, out_shape),
        scratch_shapes=scratch,
        cost_estimate=pl.CostEstimate(flops=flops, bytes_accessed=moved, transcendentals=0),
        compiler_params=pltpu.CompilerParams(vmem_limit_bytes=LIMIT),
    )


def norm_kernel(rows_ref, gain_ref, out_ref):
    rows = rows_ref[...]
    centred = rows - jnp.mean(rows, axis=-1, keepdims=True)
    spread = jnp.mean(centred * centred, axis=-1, keepdims=True)
    out_ref[...] = (centred * lax.rsqrt(spread + EPSILON) * gain_ref[...]).astype(jnp.bfloat16)


def layer_norm(rows, gain):
    return call(
        norm_kernel, jax.ShapeDtypeStruct(rows.shape, jnp.bfloat16), [VMEM, VMEM], flops=6 * rows.size, moved=6 * rows.size
    )(rows, gain)


def dot(a, b):
    return jnp.dot(a, b, preferred_element_type=jnp.float32)


def project_into(blocks, weights, outs, base):
    rows = jnp.concatenate([block[...] for block in blocks], axis=0)
    count = rows.shape[0]
    w_query, w_key, w_value, w_gate = weights
    queries, keys, values, gates = outs
    where = pl.ds(base, count)
    queries[where] = dot(rows, w_query[0]).astype(jnp.bfloat16)
    keys[where] = (dot(rows, w_key[0]) * 0.0625).astype(jnp.bfloat16)
    values[where] = dot(rows, w_value[0]).astype(jnp.bfloat16)
    gates[where] = dot(rows, w_gate[0])


def early_kernel(b0, b1, b2, b3, wq, wk, wv, wg, queries, keys, values, gates):
    project_into((b0, b1, b2, b3), (wq, wk, wv, wg), (queries, keys, values, gates), 0)


def split(value):
    high = value.astype(jnp.bfloat16)
    return high, (value - high.astype(jnp.float32)).astype(jnp.bfloat16)


def late_kernel(
    b0, b1, b2, b3, wq, wk, wv, wg, early_q, early_k, early_v, early_g, state, decay, lead, tail, keep, w_out,
    over_z, over_x, gated_late, new_state, queries, keys, values, gates,
):
    project_into((b0, b1, b2, b3), (wq, wk, wv, wg), (queries, keys, values, gates), 0)
    half = early_q.shape[0]
    rest = pl.ds(half, half)
    queries[rest] = early_q[...]
    keys[rest] = early_k[...]
    values[rest] = early_v[...]
    gates[rest] = early_g[...]
    q, k, v = queries[...], keys[...], values[...]
    scores = lax.dot_general(q, k, (((1,), (1,)), ((), ())), preferred_element_type=jnp.float32)
    weighted = (scores * decay[...]).astype(jnp.bfloat16)
    before = state[0, 0]
    high, low = split(before)
    mixed = dot(weighted, v) + (dot(q, high) + dot(q, low)) * lead[...]
    centred = mixed - jnp.mean(mixed, axis=-1, keepdims=True)
    head_out = centred * lax.rsqrt(jnp.mean(centred * centred, axis=-1, keepdims=True) + EPSILON)
    gate = gates[...]
    gated = (gate / (1.0 + jnp.exp(-gate)) * head_out).astype(jnp.bfloat16)
    partial = dot(gated[:half], w_out[0]).astype(jnp.bfloat16)
    over_z[...] = partial[: half // 2]
    over_x[...] = partial[half // 2 :]
    gated_late[...] = gated[half:]
    k_high, k_low = split(k.astype(jnp.float32) * tail[...])
    across = (((0,), (0,)), ((), ()))
    added = lax.dot_general(k_high, v, across, preferred_element_type=jnp.float32) + lax.dot_general(
        k_low, v, across, preferred_element_type=jnp.float32
    )
    new_state[0, 0] = keep[0, 0] * before + added


def out_kernel(gated, w_out, up, down, mate, own):
    count = own.shape[0]
    up[...] = dot(gated[:count], w_out[0]).astype(jnp.bfloat16)
    down[...] = dot(gated[count : 2 * count], w_out[0]).astype(jnp.bfloat16)
    mate[...] = dot(gated[2 * count : 3 * count], w_out[0]).astype(jnp.bfloat16)
    own[...] = dot(gated[3 * count :], w_out[0])


def body(inflow, fresh, states, rates, norm_gain, w_query, w_key, w_value, w_gate, w_out):
    count, width = fresh.shape
    key_size, value_size = states.shape[2:]
    group = count * lax.axis_size("tensor")
    half = group // 2
    first_section = lax.axis_index("section") == 0
    steps = jnp.array([2, 6, 4, 4, 2, 6, 0, 0], jnp.int32)
    mates = jnp.array([1, 1, 0, 1, 0, 0, 1, 0], jnp.int32)
    order = ((lax.axis_index("tensor") + steps) & 7) ^ mates
    positions = (order[:, None] * count + jnp.arange(count)[None, :]).reshape(group).astype(jnp.float32)
    log_keep = jnp.log1p(-rates)
    offsets = positions[:, None] - positions[None, :]
    decay = jnp.where(offsets >= 0, jnp.exp(jnp.maximum(offsets, 0.0) * log_keep), 0.0)
    lead = jnp.exp((positions[:, None] + 1.0) * log_keep)
    tail = jnp.exp((group - 1.0 - positions[:, None]) * log_keep)
    keep = jnp.exp(group * log_keep)
    weights = (w_query, w_key, w_value, w_gate)
    bf16, f32 = jnp.bfloat16, jnp.float32
    shape = jax.ShapeDtypeStruct
    state = states
    own_rows = inflow[0]
    for turn_index in range(2):
        own = layer_norm(own_rows, norm_gain)
        below, above, mate = shift_x(own, 1), shift_x(own, -1), swap_z(own)
        below, above, mate, held = lax.optimization_barrier((below, above, mate, own))
        mate_above, mate_below = swap_z(above), swap_z(below)
        far, far_mate = shift_x(held, 2), shift_x(mate, 2)
        early = call(
            early_kernel,
            [shape((half, key_size), bf16)] * 2 + [shape((half, value_size), bf16), shape((half, value_size), f32)],
            [VMEM] * 8,
            flops=2 * half * width * 2 * (key_size + value_size),
            moved=2 * width * 2 * (key_size + value_size),
        )(above, below, mate, own, *weights)
        over_z, over_x, gated_late, state = call(
            late_kernel,
            [shape((half // 2, width), bf16)] * 2 + [shape((half, value_size), bf16), shape(state.shape, f32)],
            [VMEM] * 16 + [SMEM, VMEM],
            flops=2 * half * width * 2 * (key_size + value_size),
            moved=2 * width * 2 * (key_size + value_size),
            scratch=[
                pltpu.VMEM((group, key_size), bf16),
                pltpu.VMEM((group, key_size), bf16),
                pltpu.VMEM((group, value_size), bf16),
                pltpu.VMEM((group, value_size), f32),
            ],
        )(mate_above, mate_below, far, far_mate, *weights, *early, state, decay, lead, tail, keep, w_out)
        via_z, via_x = swap_z(over_z), shift_x(over_x, 2)
        up, down, to_mate, mine = call(
            out_kernel,
            [shape((count, width), bf16)] * 3 + [shape((count, width), f32)],
            [VMEM, VMEM],
            flops=2 * half * value_size * width,
            moved=2 * value_size * width,
        )(gated_late, w_out)

        def add(a, b):
            return (a.astype(f32) + b.astype(f32)).astype(bf16)

        got_up = shift_x(add(up, via_z[:count]), 1)
        got_down = shift_x(add(down, via_z[count:]), -1)
        got_mate = swap_z(add(to_mate, via_x[count:]))
        own_rows = (
            own_rows
            + mine
            + via_x[:count].astype(f32)
            + got_up.astype(f32)
            + got_down.astype(f32)
            + got_mate.astype(f32)
        )
        if turn_index == 0:
            arrived = next_section(own_rows.astype(bf16))
            own_rows = jnp.where(first_section, fresh, arrived.astype(f32))
    return (own_rows[None], state)


def solution(mesh):
    in_specs = (
        P("section", "tensor", None),
        P("tensor", None),
        P("section", "tensor", None, None),
        P("section", "tensor"),
        P("section", None),
        P("section", None, "tensor"),
        P("section", None, "tensor"),
        P("section", None, "tensor"),
        P("section", None, "tensor"),
        P("section", "tensor", None),
    )
    out_specs = (P("section", "tensor", None), P("section", "tensor", None, None))
    return jax.shard_map(body, mesh=mesh, in_specs=in_specs, out_specs=out_specs, check_vma=False)
```

```python
import jax
import jax.numpy as jnp
from jax import lax
from jax.experimental import pallas as pl
from jax.experimental.pallas import tpu as pltpu
from jax.sharding import PartitionSpec as P

EPSILON = 1e-05
VMEM = pl.BlockSpec(memory_space=pltpu.VMEM)
SMEM = pl.BlockSpec(memory_space=pltpu.SMEM)
HBM = pl.BlockSpec(memory_space=pltpu.HBM)
MIB = 1024 * 1024
LIMIT = 16 * MIB
ORDER = ((1, 1), (3, 1), (2, 0), (2, 1), (1, 0), (3, 0), (0, 1), (0, 0))


def shift_x(value, steps):
    return lax.ppermute(value, "tensor", [(t, (t + 2 * steps) % 8) for t in range(8)])


def swap_z(value):
    return lax.ppermute(value, "tensor", [(t, t ^ 1) for t in range(8)])


def next_section(value):
    return lax.ppermute(value, "section", [(s, s + 1) for s in range(lax.axis_size("section") - 1)])


def shape(dims, dtype):
    return jax.ShapeDtypeStruct(tuple(dims), dtype)


def call(kernel, out_shape, in_specs, flops=0, moved=0, scratch=(), limit=LIMIT):
    return pl.pallas_call(
        kernel,
        out_shape=out_shape,
        in_specs=in_specs,
        out_specs=jax.tree.map(lambda _: VMEM, out_shape),
        scratch_shapes=scratch,
        cost_estimate=pl.CostEstimate(flops=flops, bytes_accessed=moved, transcendentals=0),
        compiler_params=pltpu.CompilerParams(vmem_limit_bytes=limit),
    )


def normed(rows, gain):
    centred = rows - jnp.mean(rows, axis=-1, keepdims=True)
    spread = jnp.mean(centred * centred, axis=-1, keepdims=True)
    return (centred * lax.rsqrt(spread + EPSILON) * gain).astype(jnp.bfloat16)


def first_norm_kernel(rows_hbm, gain_hbm, state_hbm, out_ref, state_ref, rows_ref, gain_ref, sems):
    pairs = ((rows_hbm, rows_ref), (gain_hbm, gain_ref), (state_hbm, state_ref))
    copies = [pltpu.make_async_copy(source, target, sems.at[i]) for i, (source, target) in enumerate(pairs)]
    for copy in copies:
        copy.start()
    copies[0].wait()
    copies[1].wait()
    out_ref[...] = normed(rows_ref[0], gain_ref[...])
    copies[2].wait()


def second_norm_kernel(arrived_ref, fresh_ref, gain_ref, rows_ref, out_ref):
    rows = jnp.where(lax.axis_index("section") == 0, fresh_ref[...], arrived_ref[...].astype(jnp.float32))
    rows_ref[0] = rows
    out_ref[...] = normed(rows, gain_ref[...])


def setup_kernel(
    log_keep_ref, wq_hbm, wk_hbm, wv_hbm, wg_hbm, wo_hbm, wq, wk, wv, wg, wo, decay, lead, tail, sems
):
    pairs = ((wq_hbm, wq), (wk_hbm, wk), (wv_hbm, wv), (wg_hbm, wg), (wo_hbm, wo))
    copies = [pltpu.make_async_copy(source, target, sems.at[i]) for i, (source, target) in enumerate(pairs)]
    for copy in copies:
        copy.start()
    group = decay.shape[0]
    count = group // len(ORDER)
    log_keep = log_keep_ref[0, 0]
    here = lax.axis_index("tensor")
    row = lax.broadcasted_iota(jnp.int32, (group, group), 0)
    column = lax.broadcasted_iota(jnp.int32, (group, group), 1)

    def position(index):
        block = index // count
        start = jnp.zeros_like(index)
        for place, (steps, mate) in enumerate(ORDER):
            start = jnp.where(block == place, (((here + 2 * steps) & 7) ^ mate) * count, start)
        return (start + index % count).astype(jnp.float32)

    at_row, at_column = position(row), position(column)
    offsets = at_row - at_column
    decay[...] = jnp.where(offsets >= 0, jnp.exp(jnp.maximum(offsets, 0.0) * log_keep), 0.0)
    lead[...] = jnp.exp((at_row[:, :1] + 1.0) * log_keep)
    tail[...] = jnp.exp((group - 1.0 - at_row[:, :1]) * log_keep)
    for copy in copies:
        copy.wait()


def dot(a, b):
    return jnp.dot(a, b, preferred_element_type=jnp.float32)


def dot_over(a, b, axis_a, axis_b):
    return lax.dot_general(a, b, (((axis_a,), (axis_b,)), ((), ())), preferred_element_type=jnp.float32)


def project(blocks, weights):
    rows = jnp.concatenate([block[...] for block in blocks], axis=0)
    w_query, w_key, w_value, w_gate = weights
    scale = w_key.shape[2] ** -0.5
    return (
        dot(rows, w_query[0]).astype(jnp.bfloat16),
        (dot(rows, w_key[0]) * scale).astype(jnp.bfloat16),
        dot(rows, w_value[0]).astype(jnp.bfloat16),
        dot(rows, w_gate[0]),
    )


def early_kernel(b0, b1, b2, b3, wq, wk, wv, wg, queries, keys, values, gates):
    queries[...], keys[...], values[...], gates[...] = project((b0, b1, b2, b3), (wq, wk, wv, wg))


def split(value):
    high = value.astype(jnp.bfloat16)
    return high, (value - high.astype(jnp.float32)).astype(jnp.bfloat16)


def late_kernel(
    b0, b1, b2, b3, wq, wk, wv, wg, early_q, early_k, early_v, early_g, state, decay, lead, w_out,
    over_z, over_x, gated_late, keys, values,
):
    late = project((b0, b1, b2, b3), (wq, wk, wv, wg))
    q, k, v, gate = (
        jnp.concatenate([a, b[...]], axis=0) for a, b in zip(late, (early_q, early_k, early_v, early_g))
    )
    half = early_q.shape[0]
    weighted = (dot_over(q, k, 1, 1) * decay[...]).astype(jnp.bfloat16)
    high, low = split(state[0, 0])
    mixed = dot(weighted, v) + (dot(q, high) + dot(q, low)) * lead[...]
    centred = mixed - jnp.mean(mixed, axis=-1, keepdims=True)
    head_out = centred * lax.rsqrt(jnp.mean(centred * centred, axis=-1, keepdims=True) + EPSILON)
    gated = (gate / (1.0 + jnp.exp(-gate)) * head_out).astype(jnp.bfloat16)
    partial = dot(gated[:half], w_out[0]).astype(jnp.bfloat16)
    over_z[...] = partial[: half // 2]
    over_x[...] = partial[half // 2 :]
    gated_late[...] = gated[half:]
    keys[...] = k
    values[...] = v


def out_kernel(log_keep_ref, gated, w_out, keys, values, tail, state, up, down, mate, own, new_state):
    count = own.shape[0]
    up[...] = dot(gated[:count], w_out[0]).astype(jnp.bfloat16)
    down[...] = dot(gated[count : 2 * count], w_out[0]).astype(jnp.bfloat16)
    mate[...] = dot(gated[2 * count : 3 * count], w_out[0]).astype(jnp.bfloat16)
    own[...] = dot(gated[3 * count :], w_out[0])
    high, low = split(keys[...].astype(jnp.float32) * tail[...])
    added = dot_over(high, values[...], 0, 0) + dot_over(low, values[...], 0, 0)
    keep = jnp.exp(jnp.full((1, 1), keys.shape[0], jnp.float32) * log_keep_ref[0, 0])
    new_state[0, 0] = keep * state[0, 0] + added


def relay_kernel(up, down, to_mate, via_z, via_x, up_sum, down_sum, mate_sum):
    count = up.shape[0]
    f32, bf16 = jnp.float32, jnp.bfloat16
    up_sum[...] = (up[...].astype(f32) + via_z[:count].astype(f32)).astype(bf16)
    down_sum[...] = (down[...].astype(f32) + via_z[count:].astype(f32)).astype(bf16)
    mate_sum[...] = (to_mate[...].astype(f32) + via_x[count:].astype(f32)).astype(bf16)


def sum_kernel(rows, own, via_x, got_up, got_down, got_mate, out):
    total = rows[0] + own[...] + via_x[: own.shape[0]].astype(jnp.float32)
    for part in (got_up, got_down, got_mate):
        total = total + part[...].astype(jnp.float32)
    out[...] = total.astype(out.dtype).reshape(out.shape)


def body(inflow, fresh, states, rates, norm_gain, w_query, w_key, w_value, w_gate, w_out):
    count, width = fresh.shape
    key_size, value_size = states.shape[2:]
    group = count * lax.axis_size("tensor")
    half = group // 2
    bf16, f32 = jnp.bfloat16, jnp.float32
    block = shape((count, width), bf16)
    double = shape((2 * count, width), bf16)
    log_keep = jnp.log1p(-rates)
    heavy = {"flops": 2 * half * width * 2 * (key_size + value_size), "moved": 2 * width * 2 * (key_size + value_size)}
    own, state = call(
        first_norm_kernel,
        [block, shape(states.shape, f32)],
        [HBM] * 3,
        moved=6 * count * width,
        scratch=[pltpu.VMEM(inflow.shape, f32), pltpu.VMEM(norm_gain.shape, f32), pltpu.SemaphoreType.DMA((3,))],
        limit=56 * MIB,
    )(inflow, norm_gain, states)
    rows = inflow
    for turn_index in range(2):
        above, below, mate = shift_x(own, -1), shift_x(own, 1), swap_z(own)
        if turn_index == 0:
            *weights, out_weight, decay, lead, tail = call(
                setup_kernel,
                [shape(a.shape, a.dtype) for a in (w_query, w_key, w_value, w_gate, w_out)]
                + [shape((group, group), f32), shape((group, 1), f32), shape((group, 1), f32)],
                [SMEM] + [HBM] * 5,
                moved=10 * 1024 * 1024,
                scratch=[pltpu.SemaphoreType.DMA((5,))],
                limit=42 * MIB,
                    )(log_keep, w_query, w_key, w_value, w_gate, w_out)
        above, below, mate, held, decay = lax.optimization_barrier((above, below, mate, own, decay))
        mate_above, mate_below = swap_z(above), swap_z(below)
        far, far_mate = shift_x(held, 2), shift_x(mate, 2)
        early = call(
            early_kernel,
            [shape((half, key_size), bf16)] * 2 + [shape((half, value_size), bf16), shape((half, value_size), f32)],
            [VMEM] * 8,
            **heavy,
        )(above, below, mate, own, *weights)
        over_z, over_x, gated_late, keys, values = call(
            late_kernel,
            [double] * 2
            + [shape((half, value_size), bf16), shape((group, key_size), bf16), shape((group, value_size), bf16)],
            [VMEM] * 16,
            **heavy,
        )(mate_above, mate_below, far, far_mate, *weights, *early, state, decay, lead, out_weight)
        via_x, via_z = shift_x(over_x, 2), swap_z(over_z)
        up, down, to_mate, mine, state = call(
            out_kernel,
            [block] * 3 + [shape((count, width), f32), shape(state.shape, f32)],
            [SMEM] + [VMEM] * 6,
            flops=2 * half * value_size * width,
            moved=2 * value_size * width,
        )(log_keep, gated_late, out_weight, keys, values, tail, state)
        up, down, to_mate = call(relay_kernel, [block] * 3, [VMEM] * 5, moved=8 * count * width)(
            up, down, to_mate, via_z, via_x
        )
        got_up, got_down, got_mate = shift_x(up, 1), shift_x(down, -1), swap_z(to_mate)
        parts = (rows, mine, via_x, got_up, got_down, got_mate)
        if turn_index == 0:
            result = call(sum_kernel, block, [VMEM] * 6, moved=16 * count * width)(*parts)
            arrived = next_section(result)
            rows, own = call(
                second_norm_kernel, [shape(inflow.shape, f32), block], [VMEM] * 3, moved=12 * count * width
            )(arrived, fresh, norm_gain)
        else:
            rows = call(sum_kernel, shape(inflow.shape, f32), [VMEM] * 6, moved=16 * count * width)(*parts)
    return (rows, state)


def solution(mesh):
    in_specs = (
        P("section", "tensor", None),
        P("tensor", None),
        P("section", "tensor", None, None),
        P("section", "tensor"),
        P("section", None),
        P("section", None, "tensor"),
        P("section", None, "tensor"),
        P("section", None, "tensor"),
        P("section", None, "tensor"),
        P("section", "tensor", None),
    )
    out_specs = (P("section", "tensor", None), P("section", "tensor", None, None))
    return jax.shard_map(body, mesh=mesh, in_specs=in_specs, out_specs=out_specs, check_vma=False)
```

```python
import jax
import jax.numpy as jnp
from jax import lax
from jax.experimental import pallas as pl
from jax.experimental.pallas import tpu as pltpu
from jax.sharding import PartitionSpec as P

EPSILON = 1e-05
VMEM = pl.BlockSpec(memory_space=pltpu.VMEM)
SMEM = pl.BlockSpec(memory_space=pltpu.SMEM)
HBM = pl.BlockSpec(memory_space=pltpu.HBM)
MIB = 1024 * 1024
LIMIT = 16 * MIB
ORDER = ((1, 1), (3, 1), (2, 0), (2, 1), (1, 0), (3, 0), (0, 1), (0, 0))


def shift_x(value, steps):
    return lax.ppermute(value, "tensor", [(t, (t + 2 * steps) % 8) for t in range(8)])


def swap_z(value):
    return lax.ppermute(value, "tensor", [(t, t ^ 1) for t in range(8)])


def next_section(value):
    return lax.ppermute(value, "section", [(s, s + 1) for s in range(lax.axis_size("section") - 1)])


def other_core(value):
    count = lax.axis_size("section")
    return lax.ppermute(value[:16, :128], "section", [(s, s ^ 1) for s in range(count)])


def shape(dims, dtype):
    return jax.ShapeDtypeStruct(tuple(dims), dtype)


def call(kernel, out_shape, in_specs, flops=0, moved=0, scratch=(), limit=LIMIT):
    return pl.pallas_call(
        kernel,
        out_shape=out_shape,
        in_specs=in_specs,
        out_specs=jax.tree.map(lambda _: VMEM, out_shape),
        scratch_shapes=scratch,
        cost_estimate=pl.CostEstimate(flops=flops, bytes_accessed=moved, transcendentals=0),
        compiler_params=pltpu.CompilerParams(vmem_limit_bytes=limit),
    )


def normed(rows, gain):
    centred = rows - jnp.mean(rows, axis=-1, keepdims=True)
    spread = jnp.mean(centred * centred, axis=-1, keepdims=True)
    return (centred * lax.rsqrt(spread + EPSILON) * gain).astype(jnp.bfloat16)


def first_norm_kernel(rows_hbm, gain_hbm, state_hbm, out_ref, state_ref, rows_ref, gain_ref, sems):
    pairs = ((rows_hbm, rows_ref), (gain_hbm, gain_ref), (state_hbm, state_ref))
    copies = [pltpu.make_async_copy(source, target, sems.at[i]) for i, (source, target) in enumerate(pairs)]
    for copy in copies:
        copy.start()
    copies[0].wait()
    copies[1].wait()
    out_ref[...] = normed(rows_ref[0], gain_ref[...])
    copies[2].wait()


def second_norm_kernel(arrived_ref, in_step_ref, fresh_ref, gain_ref, rows_ref, out_ref):
    rows = jnp.where(lax.axis_index("section") == 0, fresh_ref[...], arrived_ref[...].astype(jnp.float32))
    rows_ref[0] = rows
    out_ref[...] = normed(rows, gain_ref[...])


def setup_kernel(
    log_keep_ref, wq_hbm, wk_hbm, wv_hbm, wg_hbm, wo_hbm, wq, wk, wv, wg, wo, decay, lead, tail, sems
):
    pairs = ((wq_hbm, wq), (wk_hbm, wk), (wv_hbm, wv), (wg_hbm, wg), (wo_hbm, wo))
    copies = [pltpu.make_async_copy(source, target, sems.at[i]) for i, (source, target) in enumerate(pairs)]
    for copy in copies:
        copy.start()
    group = decay.shape[0]
    count = group // len(ORDER)
    log_keep = log_keep_ref[0, 0]
    here = lax.axis_index("tensor")
    row = lax.broadcasted_iota(jnp.int32, (group, group), 0)
    column = lax.broadcasted_iota(jnp.int32, (group, group), 1)

    def position(index):
        block = index // count
        start = jnp.zeros_like(index)
        for place, (steps, mate) in enumerate(ORDER):
            start = jnp.where(block == place, (((here + 2 * steps) & 7) ^ mate) * count, start)
        return (start + index % count).astype(jnp.float32)

    at_row, at_column = position(row), position(column)
    offsets = at_row - at_column
    decay[...] = jnp.where(offsets >= 0, jnp.exp(jnp.maximum(offsets, 0.0) * log_keep), 0.0)
    lead[...] = jnp.exp((at_row[:, :1] + 1.0) * log_keep)
    tail[...] = jnp.exp((group - 1.0 - at_row[:, :1]) * log_keep)
    for copy in copies:
        copy.wait()


def halves_kernel(above, below, left, right):
    width = left.shape[1]
    left[...] = above[:, :width]
    right[...] = below[:, width:]


def dot(a, b):
    return jnp.dot(a, b, preferred_element_type=jnp.float32)


def dot_over(a, b, axis_a, axis_b):
    return lax.dot_general(a, b, (((axis_a,), (axis_b,)), ((), ())), preferred_element_type=jnp.float32)


def project(blocks, weights):
    rows = jnp.concatenate([block[...] for block in blocks], axis=0)
    w_query, w_key, w_value, w_gate = weights
    scale = w_key.shape[2] ** -0.5
    return (
        dot(rows, w_query[0]).astype(jnp.bfloat16),
        (dot(rows, w_key[0]) * scale).astype(jnp.bfloat16),
        dot(rows, w_value[0]).astype(jnp.bfloat16),
        dot(rows, w_gate[0]),
    )


def early_kernel(b0, b1, b2, b3, wq, wk, wv, wg, queries, keys, values, gates):
    queries[...], keys[...], values[...], gates[...] = project((b0, b1, b2, b3), (wq, wk, wv, wg))


def split(value):
    high = value.astype(jnp.bfloat16)
    return high, (value - high.astype(jnp.float32)).astype(jnp.bfloat16)


def late_kernel(
    b0, b1, b2_left, b2_right, b3, wq, wk, wv, wg, early_q, early_k, early_v, early_g, state, decay, lead, w_out,
    over_z, over_x, half_up, half_down, gated_late, keys, values,
):
    b2 = jnp.concatenate([b2_left[...], b2_right[...]], axis=1)
    late = project((b0, b1, b2, b3), (wq, wk, wv, wg))
    q, k, v, gate = (
        jnp.concatenate([a, b[...]], axis=0) for a, b in zip(late, (early_q, early_k, early_v, early_g))
    )
    half = early_q.shape[0]
    weighted = (dot_over(q, k, 1, 1) * decay[...]).astype(jnp.bfloat16)
    high, low = split(state[0, 0])
    mixed = dot(weighted, v) + (dot(q, high) + dot(q, low)) * lead[...]
    centred = mixed - jnp.mean(mixed, axis=-1, keepdims=True)
    head_out = centred * lax.rsqrt(jnp.mean(centred * centred, axis=-1, keepdims=True) + EPSILON)
    gated = (gate / (1.0 + jnp.exp(-gate)) * head_out).astype(jnp.bfloat16)
    partial = dot(gated[:half], w_out[0]).astype(jnp.bfloat16)
    over_z[...] = partial[: half // 2]
    count, width = half_up.shape
    over_x[...] = partial[3 * count :]
    half_up[...] = partial[2 * count : 3 * count, :width]
    half_down[...] = partial[2 * count : 3 * count, width:]
    gated_late[...] = gated[half:]
    keys[...] = k
    values[...] = v


def out_kernel(log_keep_ref, gated, w_out, keys, values, tail, state, up, down, mate, own, new_state):
    count = own.shape[0]
    up[...] = dot(gated[:count], w_out[0]).astype(jnp.bfloat16)
    down[...] = dot(gated[count : 2 * count], w_out[0]).astype(jnp.bfloat16)
    mate[...] = dot(gated[2 * count : 3 * count], w_out[0]).astype(jnp.bfloat16)
    own[...] = dot(gated[3 * count :], w_out[0])
    high, low = split(keys[...].astype(jnp.float32) * tail[...])
    added = dot_over(high, values[...], 0, 0) + dot_over(low, values[...], 0, 0)
    keep = jnp.exp(jnp.full((1, 1), keys.shape[0], jnp.float32) * log_keep_ref[0, 0])
    new_state[0, 0] = keep * state[0, 0] + added


def relay_kernel(up, down, to_mate, via_z, via_x, via_up, via_down, up_sum, down_sum, mate_sum):
    f32 = jnp.float32
    count, width = via_up.shape
    up_total = up[...].astype(f32) + via_z[:count].astype(f32)
    down_total = down[...].astype(f32) + via_z[count:].astype(f32)
    up_sum[:, :width] = (up_total[:, :width] + via_up[...].astype(f32)).astype(up_sum.dtype)
    up_sum[:, width:] = up_total[:, width:].astype(up_sum.dtype)
    down_sum[:, :width] = down_total[:, :width].astype(down_sum.dtype)
    down_sum[:, width:] = (down_total[:, width:] + via_down[...].astype(f32)).astype(down_sum.dtype)
    mate_sum[...] = (to_mate[...].astype(f32) + via_x[...].astype(f32)).astype(mate_sum.dtype)


def sum_kernel(rows, own, got_up, got_down, got_mate, out):
    total = rows[0] + own[...]
    for part in (got_up, got_down, got_mate):
        total = total + part[...].astype(jnp.float32)
    out[...] = total.astype(out.dtype).reshape(out.shape)


def body(inflow, fresh, states, rates, norm_gain, w_query, w_key, w_value, w_gate, w_out):
    count, width = fresh.shape
    key_size, value_size = states.shape[2:]
    group = count * lax.axis_size("tensor")
    half = group // 2
    bf16, f32 = jnp.bfloat16, jnp.float32
    block = shape((count, width), bf16)
    double = shape((2 * count, width), bf16)
    half_block = shape((count, width // 2), bf16)
    log_keep = jnp.log1p(-rates)
    heavy = {"flops": 2 * half * width * 2 * (key_size + value_size), "moved": 2 * width * 2 * (key_size + value_size)}
    own, state = call(
        first_norm_kernel,
        [block, shape(states.shape, f32)],
        [HBM] * 3,
        moved=6 * count * width,
        scratch=[pltpu.VMEM(inflow.shape, f32), pltpu.VMEM(norm_gain.shape, f32), pltpu.SemaphoreType.DMA((3,))],
        limit=56 * MIB,
    )(inflow, norm_gain, states)
    rows = inflow
    for turn_index in range(2):
        above, below, mate = shift_x(own, -1), shift_x(own, 1), swap_z(own)
        if turn_index == 0:
            *weights, out_weight, decay, lead, tail = call(
                setup_kernel,
                [shape(a.shape, a.dtype) for a in (w_query, w_key, w_value, w_gate, w_out)]
                + [shape((group, group), f32), shape((group, 1), f32), shape((group, 1), f32)],
                [SMEM] + [HBM] * 5,
                moved=10 * 1024 * 1024,
                scratch=[pltpu.SemaphoreType.DMA((5,))],
                limit=42 * MIB,
                    )(log_keep, w_query, w_key, w_value, w_gate, w_out)
        above, below, mate, decay = lax.optimization_barrier((above, below, mate, decay))
        mate_above, mate_below = swap_z(above), swap_z(below)
        far_mate = shift_x(mate, 2)
        left, right = call(halves_kernel, [half_block] * 2, [VMEM] * 2, moved=4 * count * width)(above, below)
        far = (shift_x(left, -1), shift_x(right, 1))
        early = call(
            early_kernel,
            [shape((half, key_size), bf16)] * 2 + [shape((half, value_size), bf16), shape((half, value_size), f32)],
            [VMEM] * 8,
            **heavy,
        )(above, below, mate, own, *weights)
        over_z, over_x, half_up, half_down, gated_late, keys, values = call(
            late_kernel,
            [double, block, half_block, half_block]
            + [shape((half, value_size), bf16), shape((group, key_size), bf16), shape((group, value_size), bf16)],
            [VMEM] * 17,
            **heavy,
        )(mate_above, mate_below, *far, far_mate, *weights, *early, state, decay, lead, out_weight)
        via_z, via_x = swap_z(over_z), shift_x(over_x, 2)
        via_up, via_down = shift_x(half_up, 1), shift_x(half_down, -1)
        up, down, to_mate, mine, state = call(
            out_kernel,
            [block] * 3 + [shape((count, width), f32), shape(state.shape, f32)],
            [SMEM] + [VMEM] * 6,
            flops=2 * half * value_size * width,
            moved=2 * value_size * width,
        )(log_keep, gated_late, out_weight, keys, values, tail, state)
        up, down, to_mate = call(relay_kernel, [block] * 3, [VMEM] * 7, moved=8 * count * width)(
            up, down, to_mate, via_z, via_x, via_up, via_down
        )
        got_up, got_down, got_mate = shift_x(up, 1), shift_x(down, -1), swap_z(to_mate)
        parts = (rows, mine, got_up, got_down, got_mate)
        if turn_index == 0:
            result = call(sum_kernel, block, [VMEM] * 5, moved=16 * count * width)(*parts)
            arrived = next_section(result)
            rows, own = call(
                second_norm_kernel, [shape(inflow.shape, f32), block], [VMEM] * 4, moved=12 * count * width
            )(arrived, other_core(arrived), fresh, norm_gain)
        else:
            rows = call(sum_kernel, shape(inflow.shape, f32), [VMEM] * 5, moved=16 * count * width)(*parts)
    return (rows, state)


def solution(mesh):
    in_specs = (
        P("section", "tensor", None),
        P("tensor", None),
        P("section", "tensor", None, None),
        P("section", "tensor"),
        P("section", None),
        P("section", None, "tensor"),
        P("section", None, "tensor"),
        P("section", None, "tensor"),
        P("section", None, "tensor"),
        P("section", "tensor", None),
    )
    out_specs = (P("section", "tensor", None), P("section", "tensor", None, None))
    return jax.shard_map(body, mesh=mesh, in_specs=in_specs, out_specs=out_specs, check_vma=False)
```

```python
import jax
import jax.numpy as jnp
from jax import lax
from jax.experimental import pallas as pl
from jax.experimental.pallas import tpu as pltpu
from jax.sharding import PartitionSpec as P

EPSILON = 1e-05
VMEM = pl.BlockSpec(memory_space=pltpu.VMEM)
SMEM = pl.BlockSpec(memory_space=pltpu.SMEM)
HBM = pl.BlockSpec(memory_space=pltpu.HBM)
MIB = 1024 * 1024
LIMIT = 16 * MIB
ORDER = ((1, 1), (3, 1), (2, 0), (2, 1), (1, 0), (3, 0), (0, 1), (0, 0))


def shift_x(value, steps):
    return lax.ppermute(value, "tensor", [(t, (t + 2 * steps) % 8) for t in range(8)])


def swap_z(value):
    return lax.ppermute(value, "tensor", [(t, t ^ 1) for t in range(8)])


def next_section(value):
    return lax.ppermute(value, "section", [(s, s + 1) for s in range(lax.axis_size("section") - 1)])


def other_core(value):
    count = lax.axis_size("section")
    return lax.ppermute(value[:16, :128], "section", [(s, s ^ 1) for s in range(count)])


def shape(dims, dtype):
    return jax.ShapeDtypeStruct(tuple(dims), dtype)


def call(kernel, out_shape, in_specs, flops=0, moved=0, scratch=(), limit=LIMIT):
    return pl.pallas_call(
        kernel,
        out_shape=out_shape,
        in_specs=in_specs,
        out_specs=jax.tree.map(lambda _: VMEM, out_shape),
        scratch_shapes=scratch,
        cost_estimate=pl.CostEstimate(flops=flops, bytes_accessed=moved, transcendentals=0),
        compiler_params=pltpu.CompilerParams(vmem_limit_bytes=limit),
    )


def normed(rows, gain):
    centred = rows - jnp.mean(rows, axis=-1, keepdims=True)
    spread = jnp.mean(centred * centred, axis=-1, keepdims=True)
    return (centred * lax.rsqrt(spread + EPSILON) * gain).astype(jnp.bfloat16)


def first_norm_kernel(rows_hbm, gain_hbm, state_hbm, out_ref, state_ref, rows_ref, gain_ref, sems):
    pairs = ((rows_hbm, rows_ref), (gain_hbm, gain_ref), (state_hbm, state_ref))
    copies = [pltpu.make_async_copy(source, target, sems.at[i]) for i, (source, target) in enumerate(pairs)]
    for copy in copies:
        copy.start()
    copies[0].wait()
    copies[1].wait()
    out_ref[...] = normed(rows_ref[0], gain_ref[...])
    copies[2].wait()


def second_norm_kernel(arrived_ref, fresh_ref, gain_ref, rows_ref, out_ref):
    rows = jnp.where(lax.axis_index("section") == 0, fresh_ref[...], arrived_ref[...].astype(jnp.float32))
    rows_ref[0] = rows
    out_ref[...] = normed(rows, gain_ref[...])


def setup_kernel(
    log_keep_ref, wq_hbm, wk_hbm, wv_hbm, wg_hbm, wo_hbm, wq, wk, wv, wg, wo, decay, lead, tail, sems
):
    pairs = ((wq_hbm, wq), (wk_hbm, wk), (wv_hbm, wv), (wg_hbm, wg), (wo_hbm, wo))
    copies = [pltpu.make_async_copy(source, target, sems.at[i]) for i, (source, target) in enumerate(pairs)]
    for copy in copies:
        copy.start()
    group = decay.shape[0]
    count = group // len(ORDER)
    log_keep = log_keep_ref[0, 0]
    here = lax.axis_index("tensor")
    row = lax.broadcasted_iota(jnp.int32, (group, group), 0)
    column = lax.broadcasted_iota(jnp.int32, (group, group), 1)

    def position(index):
        block = index // count
        start = jnp.zeros_like(index)
        for place, (steps, mate) in enumerate(ORDER):
            start = jnp.where(block == place, (((here + 2 * steps) & 7) ^ mate) * count, start)
        return (start + index % count).astype(jnp.float32)

    at_row, at_column = position(row), position(column)
    offsets = at_row - at_column
    decay[...] = jnp.where(offsets >= 0, jnp.exp(jnp.maximum(offsets, 0.0) * log_keep), 0.0)
    lead[...] = jnp.exp((at_row[:, :1] + 1.0) * log_keep)
    tail[...] = jnp.exp((group - 1.0 - at_row[:, :1]) * log_keep)
    for copy in copies:
        copy.wait()


def halves_kernel(above, below, both, left, right):
    count, width = left.shape
    both[:count] = above[...]
    both[count:] = below[...]
    left[...] = above[:, :width]
    right[...] = below[:, width:]


def dot(a, b):
    return jnp.dot(a, b, preferred_element_type=jnp.float32)


def dot_over(a, b, axis_a, axis_b):
    return lax.dot_general(a, b, (((axis_a,), (axis_b,)), ((), ())), preferred_element_type=jnp.float32)


def project(blocks, weights):
    rows = jnp.concatenate([block[...] for block in blocks], axis=0)
    w_query, w_key, w_value, w_gate = weights
    scale = w_key.shape[2] ** -0.5
    return (
        dot(rows, w_query[0]).astype(jnp.bfloat16),
        (dot(rows, w_key[0]) * scale).astype(jnp.bfloat16),
        dot(rows, w_value[0]).astype(jnp.bfloat16),
        dot(rows, w_gate[0]),
    )


def early_kernel(b0, b1, b2, b3, wq, wk, wv, wg, queries, keys, values, gates):
    queries[...], keys[...], values[...], gates[...] = project((b0, b1, b2, b3), (wq, wk, wv, wg))


def split(value):
    high = value.astype(jnp.bfloat16)
    return high, (value - high.astype(jnp.float32)).astype(jnp.bfloat16)


def late_kernel(
    both, b2_left, b2_right, b3, wq, wk, wv, wg, early_q, early_k, early_v, early_g, state, decay, lead, w_out,
    over_z, over_x, half_up, half_down, gated_late, keys, values,
):
    b2 = jnp.concatenate([b2_left[...], b2_right[...]], axis=1)
    late = project((both, b2, b3), (wq, wk, wv, wg))
    q, k, v, gate = (
        jnp.concatenate([a, b[...]], axis=0) for a, b in zip(late, (early_q, early_k, early_v, early_g))
    )
    half = early_q.shape[0]
    weighted = (dot_over(q, k, 1, 1) * decay[...]).astype(jnp.bfloat16)
    high, low = split(state[0, 0])
    mixed = dot(weighted, v) + (dot(q, high) + dot(q, low)) * lead[...]
    centred = mixed - jnp.mean(mixed, axis=-1, keepdims=True)
    head_out = centred * lax.rsqrt(jnp.mean(centred * centred, axis=-1, keepdims=True) + EPSILON)
    gated = (gate / (1.0 + jnp.exp(-gate)) * head_out).astype(jnp.bfloat16)
    partial = dot(gated[:half], w_out[0]).astype(jnp.bfloat16)
    over_z[...] = partial[: half // 2]
    count, width = half_up.shape
    over_x[...] = partial[3 * count :]
    half_up[...] = partial[2 * count : 3 * count, :width]
    half_down[...] = partial[2 * count : 3 * count, width:]
    gated_late[...] = gated[half:]
    keys[...] = k
    values[...] = v


def out_kernel(log_keep_ref, gated, w_out, keys, values, tail, state, up, down, mate, own, new_state):
    count = own.shape[0]
    up[...] = dot(gated[:count], w_out[0]).astype(jnp.bfloat16)
    down[...] = dot(gated[count : 2 * count], w_out[0]).astype(jnp.bfloat16)
    mate[...] = dot(gated[2 * count : 3 * count], w_out[0]).astype(jnp.bfloat16)
    own[...] = dot(gated[3 * count :], w_out[0])
    high, low = split(keys[...].astype(jnp.float32) * tail[...])
    added = dot_over(high, values[...], 0, 0) + dot_over(low, values[...], 0, 0)
    keep = jnp.exp(jnp.full((1, 1), keys.shape[0], jnp.float32) * log_keep_ref[0, 0])
    new_state[0, 0] = keep * state[0, 0] + added


def relay_kernel(up, down, to_mate, via_z, via_x, via_up, via_down, up_sum, down_sum, mate_sum):
    f32 = jnp.float32
    count, width = via_up.shape
    up_total = up[...].astype(f32) + via_z[:count].astype(f32)
    down_total = down[...].astype(f32) + via_z[count:].astype(f32)
    up_sum[:, :width] = (up_total[:, :width] + via_up[...].astype(f32)).astype(up_sum.dtype)
    up_sum[:, width:] = up_total[:, width:].astype(up_sum.dtype)
    down_sum[:, :width] = down_total[:, :width].astype(down_sum.dtype)
    down_sum[:, width:] = (down_total[:, width:] + via_down[...].astype(f32)).astype(down_sum.dtype)
    mate_sum[...] = (to_mate[...].astype(f32) + via_x[...].astype(f32)).astype(mate_sum.dtype)


def sum_kernel(rows, own, got_up, got_down, got_mate, out):
    total = rows[0] + own[...]
    for part in (got_up, got_down, got_mate):
        total = total + part[...].astype(jnp.float32)
    out[...] = total.astype(out.dtype).reshape(out.shape)


def body(inflow, fresh, states, rates, norm_gain, w_query, w_key, w_value, w_gate, w_out):
    count, width = fresh.shape
    key_size, value_size = states.shape[2:]
    group = count * lax.axis_size("tensor")
    half = group // 2
    bf16, f32 = jnp.bfloat16, jnp.float32
    block = shape((count, width), bf16)
    double = shape((2 * count, width), bf16)
    half_block = shape((count, width // 2), bf16)
    log_keep = jnp.log1p(-rates)
    heavy = {"flops": 2 * half * width * 2 * (key_size + value_size), "moved": 2 * width * 2 * (key_size + value_size)}
    own, state = call(
        first_norm_kernel,
        [block, shape(states.shape, f32)],
        [HBM] * 3,
        moved=6 * count * width,
        scratch=[pltpu.VMEM(inflow.shape, f32), pltpu.VMEM(norm_gain.shape, f32), pltpu.SemaphoreType.DMA((3,))],
        limit=56 * MIB,
    )(inflow, norm_gain, states)
    rows = inflow
    for turn_index in range(2):
        above, below, mate = shift_x(own, -1), shift_x(own, 1), swap_z(own)
        if turn_index == 0:
            *weights, out_weight, decay, lead, tail = call(
                setup_kernel,
                [shape(a.shape, a.dtype) for a in (w_query, w_key, w_value, w_gate, w_out)]
                + [shape((group, group), f32), shape((group, 1), f32), shape((group, 1), f32)],
                [SMEM] + [HBM] * 5,
                moved=10 * 1024 * 1024,
                scratch=[pltpu.SemaphoreType.DMA((5,))],
                limit=42 * MIB,
                    )(log_keep, w_query, w_key, w_value, w_gate, w_out)
        above, below, mate, decay = lax.optimization_barrier((above, below, mate, decay))
        both, left, right = call(
            halves_kernel, [double, half_block, half_block], [VMEM] * 2, moved=12 * count * width
        )(above, below)
        late = (swap_z(both), shift_x(left, -1), shift_x(right, 1), shift_x(mate, 2))
        early = call(
            early_kernel,
            [shape((half, key_size), bf16)] * 2 + [shape((half, value_size), bf16), shape((half, value_size), f32)],
            [VMEM] * 8,
            **heavy,
        )(above, below, mate, own, *weights)
        over_z, over_x, half_up, half_down, gated_late, keys, values = call(
            late_kernel,
            [double, block, half_block, half_block]
            + [shape((half, value_size), bf16), shape((group, key_size), bf16), shape((group, value_size), bf16)],
            [VMEM] * 16,
            **heavy,
        )(*late, *weights, *early, state, decay, lead, out_weight)
        via_z, via_x = swap_z(over_z), shift_x(over_x, 2)
        via_up, via_down = shift_x(half_up, 1), shift_x(half_down, -1)
        up, down, to_mate, mine, state = call(
            out_kernel,
            [block] * 3 + [shape((count, width), f32), shape(state.shape, f32)],
            [SMEM] + [VMEM] * 6,
            flops=2 * half * value_size * width,
            moved=2 * value_size * width,
        )(log_keep, gated_late, out_weight, keys, values, tail, state)
        up, down, to_mate = call(relay_kernel, [block] * 3, [VMEM] * 7, moved=8 * count * width)(
            up, down, to_mate, via_z, via_x, via_up, via_down
        )
        got_up, got_down, got_mate = shift_x(up, 1), shift_x(down, -1), swap_z(to_mate)
        parts = (rows, mine, got_up, got_down, got_mate)
        if turn_index == 0:
            result = call(sum_kernel, block, [VMEM] * 5, moved=16 * count * width)(*parts)
            arrived = next_section(result)
            rows, own = call(
                second_norm_kernel, [shape(inflow.shape, f32), block], [VMEM] * 3, moved=12 * count * width
            )(arrived, fresh, norm_gain)
        else:
            rows = call(sum_kernel, shape(inflow.shape, f32), [VMEM] * 5, moved=16 * count * width)(*parts)
    return (rows, state)


def solution(mesh):
    in_specs = (
        P("section", "tensor", None),
        P("tensor", None),
        P("section", "tensor", None, None),
        P("section", "tensor"),
        P("section", None),
        P("section", None, "tensor"),
        P("section", None, "tensor"),
        P("section", None, "tensor"),
        P("section", None, "tensor"),
        P("section", "tensor", None),
    )
    out_specs = (P("section", "tensor", None), P("section", "tensor", None, None))
    return jax.shard_map(body, mesh=mesh, in_specs=in_specs, out_specs=out_specs, check_vma=False)
```

```python
import jax
import jax.numpy as jnp
from jax import lax
from jax.experimental import pallas as pl
from jax.experimental.pallas import tpu as pltpu
from jax.sharding import PartitionSpec as P

EPSILON = 1e-05
VMEM = pl.BlockSpec(memory_space=pltpu.VMEM)
SMEM = pl.BlockSpec(memory_space=pltpu.SMEM)
HBM = pl.BlockSpec(memory_space=pltpu.HBM)
MIB = 1024 * 1024
LIMIT = 16 * MIB
ORDER = ((1, 1), (3, 1), (2, 0), (2, 1), (1, 0), (3, 0), (0, 1), (0, 0))


def shift_x(value, steps):
    return lax.ppermute(value, "tensor", [(t, (t + 2 * steps) % 8) for t in range(8)])


def swap_z(value):
    return lax.ppermute(value, "tensor", [(t, t ^ 1) for t in range(8)])


def next_section(value):
    return lax.ppermute(value, "section", [(s, s + 1) for s in range(lax.axis_size("section") - 1)])


def other_core(value):
    count = lax.axis_size("section")
    return lax.ppermute(value[:16, :128], "section", [(s, s ^ 1) for s in range(count)])


def shape(dims, dtype):
    return jax.ShapeDtypeStruct(tuple(dims), dtype)


def call(kernel, out_shape, in_specs, flops=0, moved=0, scratch=(), limit=LIMIT):
    return pl.pallas_call(
        kernel,
        out_shape=out_shape,
        in_specs=in_specs,
        out_specs=jax.tree.map(lambda _: VMEM, out_shape),
        scratch_shapes=scratch,
        cost_estimate=pl.CostEstimate(flops=flops, bytes_accessed=moved, transcendentals=0),
        compiler_params=pltpu.CompilerParams(vmem_limit_bytes=limit),
    )


def normed(rows, gain):
    centred = rows - jnp.mean(rows, axis=-1, keepdims=True)
    spread = jnp.mean(centred * centred, axis=-1, keepdims=True)
    return (centred * lax.rsqrt(spread + EPSILON) * gain).astype(jnp.bfloat16)


def first_norm_kernel(rows_hbm, gain_hbm, state_hbm, out_ref, state_ref, rows_ref, gain_ref, sems):
    pairs = ((rows_hbm, rows_ref), (gain_hbm, gain_ref), (state_hbm, state_ref))
    copies = [pltpu.make_async_copy(source, target, sems.at[i]) for i, (source, target) in enumerate(pairs)]
    for copy in copies:
        copy.start()
    copies[0].wait()
    copies[1].wait()
    out_ref[...] = normed(rows_ref[0], gain_ref[...])
    copies[2].wait()


def second_norm_kernel(arrived_ref, fresh_ref, gain_ref, rows_ref, out_ref):
    rows = jnp.where(lax.axis_index("section") == 0, fresh_ref[...], arrived_ref[...].astype(jnp.float32))
    rows_ref[0] = rows
    out_ref[...] = normed(rows, gain_ref[...])


def setup_kernel(
    log_keep_ref, wq_hbm, wk_hbm, wv_hbm, wg_hbm, wo_hbm, wq, wk, wv, wg, wo, decay, lead, tail, sems
):
    pairs = ((wq_hbm, wq), (wk_hbm, wk), (wv_hbm, wv), (wg_hbm, wg), (wo_hbm, wo))
    copies = [pltpu.make_async_copy(source, target, sems.at[i]) for i, (source, target) in enumerate(pairs)]
    for copy in copies:
        copy.start()
    group = decay.shape[0]
    count = group // len(ORDER)
    log_keep = log_keep_ref[0, 0]
    here = lax.axis_index("tensor")
    row = lax.broadcasted_iota(jnp.int32, (group, group), 0)
    column = lax.broadcasted_iota(jnp.int32, (group, group), 1)

    def position(index):
        block = index // count
        start = jnp.zeros_like(index)
        for place, (steps, mate) in enumerate(ORDER):
            start = jnp.where(block == place, (((here + 2 * steps) & 7) ^ mate) * count, start)
        return (start + index % count).astype(jnp.float32)

    at_row, at_column = position(row), position(column)
    offsets = at_row - at_column
    decay[...] = jnp.where(offsets >= 0, jnp.exp(jnp.maximum(offsets, 0.0) * log_keep), 0.0)
    lead[...] = jnp.exp((at_row[:, :1] + 1.0) * log_keep)
    tail[...] = jnp.exp((group - 1.0 - at_row[:, :1]) * log_keep)
    for copy in copies:
        copy.wait()


def halves_kernel(above, below, both, left, right):
    count, width = left.shape
    both[:count] = above[...]
    both[count:] = below[...]
    left[...] = above[:, :width]
    right[...] = below[:, width:]


def dot(a, b):
    return jnp.dot(a, b, preferred_element_type=jnp.float32)


def dot_over(a, b, axis_a, axis_b):
    return lax.dot_general(a, b, (((axis_a,), (axis_b,)), ((), ())), preferred_element_type=jnp.float32)


def project(blocks, weights):
    rows = jnp.concatenate([block[...] for block in blocks], axis=0)
    w_query, w_key, w_value, w_gate = weights
    scale = w_key.shape[2] ** -0.5
    return (
        dot(rows, w_query[0]).astype(jnp.bfloat16),
        (dot(rows, w_key[0]) * scale).astype(jnp.bfloat16),
        dot(rows, w_value[0]).astype(jnp.bfloat16),
        dot(rows, w_gate[0]),
    )


def early_kernel(b0, b1, b2, b3, wq, wk, wv, wg, queries, keys, values, gates):
    queries[...], keys[...], values[...], gates[...] = project((b0, b1, b2, b3), (wq, wk, wv, wg))


def split(value):
    high = value.astype(jnp.bfloat16)
    return high, (value - high.astype(jnp.float32)).astype(jnp.bfloat16)


def late_kernel(
    both, b2_left, b2_right, b3, wq, wk, wv, wg, early_q, early_k, early_v, early_g, state, decay, lead, w_out,
    over_z, over_x, half_up, half_down, gated_late, keys, values,
):
    b2 = jnp.concatenate([b2_left[...], b2_right[...]], axis=1)
    late = project((both, b2, b3), (wq, wk, wv, wg))
    q, k, v, gate = (
        jnp.concatenate([a, b[...]], axis=0) for a, b in zip(late, (early_q, early_k, early_v, early_g))
    )
    half = early_q.shape[0]
    weighted = (dot_over(q, k, 1, 1) * decay[...]).astype(jnp.bfloat16)
    high, low = split(state[0, 0])
    mixed = dot(weighted, v) + (dot(q, high) + dot(q, low)) * lead[...]
    centred = mixed - jnp.mean(mixed, axis=-1, keepdims=True)
    head_out = centred * lax.rsqrt(jnp.mean(centred * centred, axis=-1, keepdims=True) + EPSILON)
    gated = (gate / (1.0 + jnp.exp(-gate)) * head_out).astype(jnp.bfloat16)
    partial = dot(gated[:half], w_out[0]).astype(jnp.bfloat16)
    over_z[...] = partial[: half // 2]
    count, width = half_up.shape
    over_x[...] = partial[3 * count :]
    half_up[...] = partial[2 * count : 3 * count, :width]
    half_down[...] = partial[2 * count : 3 * count, width:]
    gated_late[...] = gated[half:]
    keys[...] = k
    values[...] = v


def out_kernel(log_keep_ref, gated, w_out, keys, values, tail, state, up, down, mate, own, new_state):
    count = own.shape[0]
    up[...] = dot(gated[:count], w_out[0]).astype(jnp.bfloat16)
    down[...] = dot(gated[count : 2 * count], w_out[0]).astype(jnp.bfloat16)
    mate[...] = dot(gated[2 * count : 3 * count], w_out[0]).astype(jnp.bfloat16)
    own[...] = dot(gated[3 * count :], w_out[0])
    high, low = split(keys[...].astype(jnp.float32) * tail[...])
    added = dot_over(high, values[...], 0, 0) + dot_over(low, values[...], 0, 0)
    keep = jnp.exp(jnp.full((1, 1), keys.shape[0], jnp.float32) * log_keep_ref[0, 0])
    new_state[0, 0] = keep * state[0, 0] + added


def relay_mate_kernel(to_mate, via_x, mate_sum):
    mate_sum[...] = (to_mate[...].astype(jnp.float32) + via_x[...].astype(jnp.float32)).astype(mate_sum.dtype)


def relay_kernel(up, down, via_z, via_up, via_down, up_sum, down_sum):
    f32 = jnp.float32
    count, width = via_up.shape
    up_total = up[...].astype(f32) + via_z[:count].astype(f32)
    down_total = down[...].astype(f32) + via_z[count:].astype(f32)
    up_sum[:, :width] = (up_total[:, :width] + via_up[...].astype(f32)).astype(up_sum.dtype)
    up_sum[:, width:] = up_total[:, width:].astype(up_sum.dtype)
    down_sum[:, :width] = down_total[:, :width].astype(down_sum.dtype)
    down_sum[:, width:] = (down_total[:, width:] + via_down[...].astype(f32)).astype(down_sum.dtype)


def sum_kernel(rows, own, got_up, got_down, got_mate, out):
    total = rows[0] + own[...]
    for part in (got_up, got_down, got_mate):
        total = total + part[...].astype(jnp.float32)
    out[...] = total.astype(out.dtype).reshape(out.shape)


def body(inflow, fresh, states, rates, norm_gain, w_query, w_key, w_value, w_gate, w_out):
    count, width = fresh.shape
    key_size, value_size = states.shape[2:]
    group = count * lax.axis_size("tensor")
    half = group // 2
    bf16, f32 = jnp.bfloat16, jnp.float32
    block = shape((count, width), bf16)
    double = shape((2 * count, width), bf16)
    half_block = shape((count, width // 2), bf16)
    log_keep = jnp.log1p(-rates)
    heavy = {"flops": 2 * half * width * 2 * (key_size + value_size), "moved": 2 * width * 2 * (key_size + value_size)}
    own, state = call(
        first_norm_kernel,
        [block, shape(states.shape, f32)],
        [HBM] * 3,
        moved=6 * count * width,
        scratch=[pltpu.VMEM(inflow.shape, f32), pltpu.VMEM(norm_gain.shape, f32), pltpu.SemaphoreType.DMA((3,))],
        limit=56 * MIB,
    )(inflow, norm_gain, states)
    rows = inflow
    for turn_index in range(2):
        above, below, mate = shift_x(own, -1), shift_x(own, 1), swap_z(own)
        if turn_index == 0:
            *weights, out_weight, decay, lead, tail = call(
                setup_kernel,
                [shape(a.shape, a.dtype) for a in (w_query, w_key, w_value, w_gate, w_out)]
                + [shape((group, group), f32), shape((group, 1), f32), shape((group, 1), f32)],
                [SMEM] + [HBM] * 5,
                moved=10 * 1024 * 1024,
                scratch=[pltpu.SemaphoreType.DMA((5,))],
                limit=42 * MIB,
                    )(log_keep, w_query, w_key, w_value, w_gate, w_out)
        above, below, mate, decay = lax.optimization_barrier((above, below, mate, decay))
        both, left, right = call(
            halves_kernel, [double, half_block, half_block], [VMEM] * 2, moved=12 * count * width
        )(above, below)
        late = (swap_z(both), shift_x(left, -1), shift_x(right, 1), shift_x(mate, 2))
        early = call(
            early_kernel,
            [shape((half, key_size), bf16)] * 2 + [shape((half, value_size), bf16), shape((half, value_size), f32)],
            [VMEM] * 8,
            **heavy,
        )(above, below, mate, own, *weights)
        over_z, over_x, half_up, half_down, gated_late, keys, values = call(
            late_kernel,
            [double, block, half_block, half_block]
            + [shape((half, value_size), bf16), shape((group, key_size), bf16), shape((group, value_size), bf16)],
            [VMEM] * 16,
            **heavy,
        )(*late, *weights, *early, state, decay, lead, out_weight)
        via_z, via_x = swap_z(over_z), shift_x(over_x, 2)
        via_up, via_down = shift_x(half_up, 1), shift_x(half_down, -1)
        up, down, to_mate, mine, state = call(
            out_kernel,
            [block] * 3 + [shape((count, width), f32), shape(state.shape, f32)],
            [SMEM] + [VMEM] * 6,
            flops=2 * half * value_size * width,
            moved=2 * value_size * width,
        )(log_keep, gated_late, out_weight, keys, values, tail, state)
        to_mate = call(relay_mate_kernel, block, [VMEM] * 2, moved=6 * count * width)(to_mate, via_x)
        got_mate = swap_z(to_mate)
        up, down = call(relay_kernel, [block] * 2, [VMEM] * 5, moved=8 * count * width)(up, down, via_z, via_up, via_down)
        got_up, got_down = shift_x(up, 1), shift_x(down, -1)
        parts = (rows, mine, got_up, got_down, got_mate)
        if turn_index == 0:
            result = call(sum_kernel, block, [VMEM] * 5, moved=16 * count * width)(*parts)
            arrived = next_section(result)
            rows, own = call(
                second_norm_kernel, [shape(inflow.shape, f32), block], [VMEM] * 3, moved=12 * count * width
            )(arrived, fresh, norm_gain)
        else:
            rows = call(sum_kernel, shape(inflow.shape, f32), [VMEM] * 5, moved=16 * count * width)(*parts)
    return (rows, state)


def solution(mesh):
    in_specs = (
        P("section", "tensor", None),
        P("tensor", None),
        P("section", "tensor", None, None),
        P("section", "tensor"),
        P("section", None),
        P("section", None, "tensor"),
        P("section", None, "tensor"),
        P("section", None, "tensor"),
        P("section", None, "tensor"),
        P("section", "tensor", None),
    )
    out_specs = (P("section", "tensor", None), P("section", "tensor", None, None))
    return jax.shard_map(body, mesh=mesh, in_specs=in_specs, out_specs=out_specs, check_vma=False)
```
